32 devices in a mesh: dp: 4 (over y, core), tensor: 8 (over z, x).
Axes of the slice: x: 2, y: 2, z: 4, core: 2. Of those that a mesh axis runs over, the one named last changes fastest.
Arguments:
- tokens: bfloat16 [1024, 8192], P('dp'), may hold values from -6 to 6
- gate_weight: bfloat16 [8192, 14336], P('dp', 'tensor'), may hold values from -0.0625 to 0.0625
- up_weight: bfloat16 [8192, 14336], P('dp', 'tensor'), may hold values from -0.0625 to 0.0625
- test_matrix: bfloat16 [14336, 512], P('tensor'), may hold values from -6 to 6
- sketch_old: float32 [14336, 512], P('tensor', 'dp'), may hold values from -6 to 6
Outputs:
- sketch_new: float32 [14336, 512], P('tensor', 'dp')
The draws below stay inside these ranges and needn't reach their ends.
All inputs are finite; a program needn't handle non-finite values.
Results may differ from the reference program's by a relative error of at most 0.02.
Values may be sent and summed in bfloat16 or wider, within the bound.
A program may use at most 128 MiB of HBM per device.

```python
import jax
import jax.numpy as jnp
from jax import lax

D = 8192
FF = 14336
R = 512
TOKENS = 1024
DBLK = 2048


def levels(key, extent, pieces, smallest, top_value):
    level = 1.0
    for dim, shards_of in pieces:
        steps = jax.random.uniform(jax.random.fold_in(jax.random.fold_in(key, 6), dim), (shards_of,), jnp.float32, smallest / len(pieces), top_value / len(pieces))
        level = level * jnp.repeat(jnp.exp(steps), extent[dim] // shards_of).reshape((-1,) + (1,) * (len(extent) - 1 - dim))
    return level


def scatter_about(own_key, shape, spread, reach, pieces=(), kind=jnp.bfloat16):
    loudness = levels(own_key, shape, pieces, -0.22, 0.18) if pieces else 1.0
    result = jax.random.normal(own_key, shape, jnp.float32) * spread * loudness
    return jnp.minimum(jnp.maximum(result, -reach), reach).astype(kind)


def setup_inputs(seed: int = 0) -> dict:
    arg_keys = jax.random.split(jax.random.key(seed), 6)
    return {
        "tokens": scatter_about(arg_keys[0], (TOKENS, D), 1.0, 6.0, ((0, 4),)),
        "gate_weight": scatter_about(arg_keys[1], (D, FF), D ** -0.5, 0.0625, ((0, 4), (1, 8))),
        "up_weight": scatter_about(arg_keys[2], (D, FF), D ** -0.5, 0.0625, ((0, 4), (1, 8))),
        "test_matrix": scatter_about(arg_keys[3], (FF, R), 1.0, 6.0, ((0, 8),)),
        "sketch_old": scatter_about(arg_keys[4], (FF, R), 1.0, 6.0, ((0, 8), (1, 4)), jnp.float32),
    }


def block_sum(tokens, weight):
    total = jnp.zeros((tokens.shape[0], weight.shape[1]), jnp.float32)
    for block in range(D // DBLK):
        first = block * DBLK
        term = jnp.dot(tokens[:, first:first + DBLK], weight[first:first + DBLK], preferred_element_type=jnp.float32)
        term = lax.optimization_barrier(term.astype(jnp.bfloat16))
        total = total + term.astype(jnp.float32)
    return total


def reference(tokens, gate_weight, up_weight, test_matrix, sketch_old):
    gate = block_sum(tokens, gate_weight)
    up = block_sum(tokens, up_weight)
    hidden = (jax.nn.silu(gate) * up).astype(jnp.bfloat16)
    projected = jnp.dot(hidden, test_matrix, preferred_element_type=jnp.float32).astype(jnp.bfloat16)
    update = lax.dot_general(hidden, projected, (((0,), (0,)), ((), ())), preferred_element_type=jnp.float32)
    return sketch_old + update / TOKENS
```

```python
import jax
import jax.numpy as jnp
from jax import lax
from jax.sharding import PartitionSpec as P


def local(tokens, gate_weight, up_weight, test_matrix, sketch_old):
    ndp = lax.axis_size("dp")
    nt = lax.axis_size("tensor")
    rows, feats = tokens.shape
    width = gate_weight.shape[1]
    t = lax.axis_index("tensor")
    d = lax.axis_index("dp")
    core = d % 2
    chip = d // 2
    chips = ndp // 2
    share = rows // nt
    part = lax.dynamic_slice_in_dim(tokens, t * share, share, axis=0)
    part = lax.all_to_all(part, "dp", split_axis=1, concat_axis=0, tiled=True)
    full = lax.all_gather(part, "tensor", axis=0, tiled=True)
    gate = jnp.dot(full, gate_weight, preferred_element_type=jnp.float32).astype(jnp.bfloat16)
    up = jnp.dot(full, up_weight, preferred_element_type=jnp.float32).astype(jnp.bfloat16)
    pairs = [(i, i ^ 1) for i in range(ndp)]
    groups = [[2 * k + c for k in range(chips)] for c in range(2)]

    def reduce(term):
        q = term.reshape(chips, 2, rows, width)
        theirs = lax.dynamic_index_in_dim(q, 1 - core, axis=1, keepdims=False)
        mine = lax.dynamic_index_in_dim(q, core, axis=1, keepdims=False)
        got = lax.ppermute(theirs, "dp", pairs)
        both = (mine.astype(jnp.float32) + got.astype(jnp.float32)).astype(jnp.bfloat16)
        if chips == 1:
            return both[0].astype(jnp.float32)
        both = lax.all_to_all(both, "dp", split_axis=0, concat_axis=0, axis_index_groups=groups)
        return jnp.sum(both.astype(jnp.float32), axis=0)

    g = reduce(gate)
    u = reduce(up)
    hidden = (jax.nn.silu(g) * u).astype(jnp.bfloat16)
    partial_proj = jnp.dot(hidden, test_matrix, preferred_element_type=jnp.float32)
    projected = lax.psum(partial_proj.astype(jnp.bfloat16), "tensor")
    local_update = lax.dot_general(
        hidden, projected, (((0,), (0,)), ((), ())), preferred_element_type=jnp.float32
    )
    summed = lax.psum_scatter(
        local_update.astype(jnp.bfloat16), "dp", scatter_dimension=1, tiled=True
    ).astype(jnp.float32)
    return sketch_old + summed / (rows * ndp)


def solution(mesh):
    in_specs = (
        P("dp", None),
        P("dp", "tensor"),
        P("dp", "tensor"),
        P("tensor", None),
        P("tensor", "dp"),
    )
    out_specs = P("tensor", "dp")
    return jax.shard_map(local, mesh=mesh, in_specs=in_specs, out_specs=out_specs, check_vma=False)
```

```python
import functools

import jax
import jax.numpy as jnp
from jax import lax
from jax.experimental import pallas as pl
from jax.experimental.pallas import tpu as pltpu
from jax.sharding import PartitionSpec as P

F32 = jnp.float32
BF16 = jnp.bfloat16


def kernel(
    ndp, nt, cw, tokens, wg, wu, test_hbm, old_hbm, out,
    xs, wv, test, old, acc, score, rcore, sy, ry, hid, proj, pstage, precv, pfull,
    u32, us, ur, us2, ur2,
    s_load, s_w, s_own, pt_s, pt_r, yt_s, yt_r, ag_s, ag_r, c_s, c_r, y_s, y_r,
    p_s, p_r, q_s, q_r, uc_s, uc_r, uy_s, uy_r,
):
    chips = ndp // 2
    rows = tokens.shape[0]
    blk, width = wg.shape
    nj = width // cw
    share = rows // nt
    steps = nt.bit_length() - 1
    d = lax.axis_index("dp")
    t = lax.axis_index("tensor")
    y = d // 2
    c = d % 2
    partner = 2 * y + 1 - c

    def rc(src, dst, ssem, rsem, dd, tt):
        return pltpu.make_async_remote_copy(
            src_ref=src, dst_ref=dst, send_sem=ssem, recv_sem=rsem,
            device_id=(dd, tt), device_id_type=pl.DeviceIdType.MESH,
        )

    def wload(j, h):
        src = (wg, wu)[h].at[:, pl.ds(pl.multiple_of(j * cw, cw), cw)]
        return pltpu.make_async_copy(src, wv.at[j, :, pl.ds(h * cw, cw)], s_w.at[h, j])

    own = pltpu.make_async_copy(
        tokens.at[:, pl.ds(pl.multiple_of(d * blk, blk), blk)],
        xs.at[y, pl.ds(pl.multiple_of(c * rows, rows), rows), :], s_own)
    own.start()
    for h in range(2):
        wload(0, h).start()

    barrier = pltpu.get_barrier_semaphore()
    for off in range(1, ndp):
        pl.semaphore_signal(barrier, inc=1, device_id=(lax.rem(d + off, ndp), t),
                            device_id_type=pl.DeviceIdType.MESH)
    for off in range(1, nt):
        pl.semaphore_signal(barrier, inc=1, device_id=(d, lax.rem(t + off, nt)),
                            device_id_type=pl.DeviceIdType.MESH)
    pl.semaphore_wait(barrier, ndp - 1 + nt - 1)

    orders = [[nt >> (k + 1) for k in range(steps)]]
    orders.append([1] + orders[0][:-1])

    def position(order):
        return sum(((t // b) % 2) * (1 << k) for k, b in enumerate(order))

    pos = [position(o) for o in orders]
    mypos = pos[0] * (1 - c) + pos[1] * c

    def region(s, cc, first, count):
        start = pl.multiple_of(cc * rows + first * share, share)
        return xs.at[s, pl.ds(start, count * share), :]

    to_partner = rc(
        tokens.at[:, pl.ds(pl.multiple_of(partner * blk, blk), blk)],
        xs.at[y, pl.ds(pl.multiple_of(c * rows, rows), rows), :],
        pt_s, pt_r, partner, t)
    to_partner.start()
    from_partner = rc(
        tokens.at[:, pl.ds(pl.multiple_of(partner * blk, blk), blk)],
        xs.at[y, pl.ds(pl.multiple_of((1 - c) * rows, rows), rows), :],
        pt_s, pt_r, partner, t)

    def token_send(i, e):
        q = 2 * lax.rem(y + i, chips) + lax.rem(c + e, 2)
        return rc(
            tokens.at[pl.ds(pl.multiple_of(mypos * share, share), share),
                      pl.ds(pl.multiple_of(q * blk, blk), blk)],
            region(y, c, mypos, 1), yt_s.at[i - 1, e], yt_r.at[i - 1, e], q, t)

    def token_recv(i, cc):
        s = lax.rem(y - i + chips, chips)
        e = lax.rem(c + cc, 2)
        ref = region(s, cc, pos[cc], 1)
        return rc(ref, ref, yt_s.at[i - 1, e], yt_r.at[i - 1, e], partner, t)

    for i in range(1, chips):
        for e in range(2):
            token_send(i, e).start()

    def gather_peer(cc, k):
        b = orders[cc][k]
        return t + (1 - 2 * ((t // b) % 2)) * b

    def gather_send(i, cc, k):
        s = lax.rem(y - i + chips, chips)
        first = (pos[cc] // (1 << k)) * (1 << k)
        ref = region(s, cc, first, 1 << k)
        return rc(ref, ref, ag_s.at[i - 1, cc, k], ag_r.at[i - 1, cc, k], d, gather_peer(cc, k))

    def gather_recv(i, cc, k):
        s = lax.rem(y - i + chips, chips)
        mine = pos[cc] // (1 << k)
        first = (mine + 1 - 2 * (mine % 2)) * (1 << k)
        ref = region(s, cc, first, 1 << k)
        return rc(ref, ref, ag_s.at[i - 1, cc, k], ag_r.at[i - 1, cc, k], d, gather_peer(cc, k))

    for j in range(1, nj):
        for h in range(2):
            wload(j, h).start()
    load_test = pltpu.make_async_copy(test_hbm, test, s_load.at[0])
    load_old = pltpu.make_async_copy(old_hbm, old, s_load.at[1])
    load_test.start()
    load_old.start()

    mine_rows = pl.ds(pl.multiple_of(c * rows, rows), rows)
    their_rows = pl.ds(pl.multiple_of((1 - c) * rows, rows), rows)

    def core_copy(i, j):
        return rc(score.at[i, j], rcore.at[i, j], c_s.at[i, j], c_r.at[i, j], partner, t)

    def y_copy(i, j):
        q = 2 * lax.rem(y + i + 1, chips) + c
        return rc(sy.at[i, j], ry.at[i, j], y_s.at[i, j], y_r.at[i, j], q, t)

    own.wait()
    from_partner.wait_recv()
    proj[...] = jnp.zeros_like(proj)
    half = (nj - 1) // 2

    for i in range(chips):
        s = lax.rem(y + i, chips)
        last = i == chips - 1

        def handle(j, i=i, last=last):
            core_copy(i, j).wait_recv()
            total = acc[j % 2, mine_rows, :] + rcore[i, j].astype(F32)
            if not last:
                sy[i, j] = total.astype(BF16)
                y_copy(i, j).start()
                return
            for k in range(chips - 1):
                y_copy(k, j).wait_recv()
                total = total + ry[k, j].astype(F32)
            gate = total[:, :cw]
            up = total[:, cw:]
            h = (gate / (1.0 + jnp.exp(-gate)) * up).astype(BF16)
            hid[j] = h
            proj[...] += jnp.dot(
                h, test[pl.ds(pl.multiple_of(j * cw, cw), cw), :], preferred_element_type=F32)

        if last:
            load_test.wait()

        def body(j, carry, i=i, s=s, handle=handle):
            if i == 0:
                for h in range(2):
                    wload(j, h).wait()
            acc[j % 2] = jnp.dot(xs[s], wv[j], preferred_element_type=F32)
            score[i, j] = acc[j % 2, their_rows, :].astype(BF16)
            core_copy(i, j).start()

            @pl.when(j > 0)
            def _():
                handle(j - 1)

            if i == 0 and chips > 1:
                @pl.when(j == half)
                def _():
                    for k in range(1, chips):
                        for cc in range(2):
                            token_recv(k, cc).wait_recv()
                            gather_send(k, cc, 0).start()
            return carry

        lax.fori_loop(0, nj, body, 0)
        handle(nj - 1)

        if i == 0 and chips > 1:
            for k in range(steps):
                for n in range(1, chips):
                    for cc in range(2):
                        gather_recv(n, cc, k).wait_recv()
                        if k + 1 < steps:
                            gather_send(n, cc, k + 1).start()

    for o in range(nt):
        pstage[o] = proj[o * share:(o + 1) * share, :].astype(BF16)

    def p_copy(off):
        tt = lax.rem(t + off, nt)
        return rc(pstage.at[tt], precv.at[off - 1], p_s.at[off - 1], p_r.at[off - 1], d, tt)

    def q_copy(off):
        tt = lax.rem(t + off, nt)
        return rc(pfull.at[t], pfull.at[t], q_s.at[off - 1], q_r.at[off - 1], d, tt)

    def q_recv(off):
        ref = pfull.at[lax.rem(t - off + nt, nt)]
        return rc(ref, ref, q_s.at[off - 1], q_r.at[off - 1], d, lax.rem(t + off, nt))

    for off in range(1, nt):
        p_copy(off).start()
    total = proj[pl.ds(pl.multiple_of(t * share, share), share), :]
    for off in range(1, nt):
        p_copy(off).wait_recv()
        total = total + precv[off - 1].astype(F32)
    pfull[t] = total.astype(BF16)
    for off in range(1, nt):
        q_copy(off).start()
    for off in range(1, nt):
        q_recv(off).wait_recv()

    oc = out.shape[1]

    def uc_copy(j):
        return rc(us.at[1 - c, j], ur.at[j], uc_s.at[j], uc_r.at[j], partner, t)

    def uy_copy(i, j):
        q = 2 * lax.rem(y + i, chips) + c
        return rc(us2.at[i - 1, j], ur2.at[i - 1, j], uy_s.at[i - 1, j], uy_r.at[i - 1, j], q, t)

    def u_handle(j):
        uc_copy(j).wait_recv()
        for i in range(1, chips):
            yy = lax.rem(y + i, chips)
            us2[i - 1, j] = (u32[c, j, yy] + ur[j, yy].astype(F32)).astype(BF16)
            uy_copy(i, j).start()

    def u_body(j, carry):
        full = pfull[...].reshape(rows, pfull.shape[2])
        r = lax.dot_general(hid[j], full, (((0,), (0,)), ((), ())), preferred_element_type=F32)
        for q in range(ndp):
            piece = r[:, q * oc:(q + 1) * oc]
            u32[q % 2, j, q // 2] = piece
            us[q % 2, j, q // 2] = piece.astype(BF16)
        uc_copy(j).start()

        @pl.when(j > 0)
        def _():
            u_handle(j - 1)
        return carry

    lax.fori_loop(0, nj, u_body, 0)
    u_handle(nj - 1)
    load_old.wait()
    scale = 1.0 / (rows * ndp)

    def o_body(j, carry):
        total = u32[c, j, y] + ur[j, y].astype(F32)
        for i in range(1, chips):
            uy_copy(i, j).wait_recv()
            total = total + ur2[i - 1, j].astype(F32)
        at = pl.ds(pl.multiple_of(j * cw, cw), cw)
        out[at, :] = old[at, :] + total * scale
        return carry

    lax.fori_loop(0, nj, o_body, 0)

    to_partner.wait_send()
    for i in range(1, chips):
        for e in range(2):
            token_send(i, e).wait_send()
            for k in range(steps):
                gather_send(i, e, k).wait_send()

    def w_body(j, carry):
        for i in range(chips):
            core_copy(i, j).wait_send()
            if i < chips - 1:
                y_copy(i, j).wait_send()
                uy_copy(i + 1, j).wait_send()
        uc_copy(j).wait_send()
        return carry

    lax.fori_loop(0, nj, w_body, 0)
    for off in range(1, nt):
        p_copy(off).wait_send()
        q_copy(off).wait_send()


def local(ndp, nt, tokens, gate_weight, up_weight, test_matrix, sketch_old):
    rows = tokens.shape[0]
    blk, width = gate_weight.shape
    rank = test_matrix.shape[1]
    oc = sketch_old.shape[1]
    cw = 256 if width % 256 == 0 else 128
    nj = width // cw
    chips = ndp // 2
    oth = max(chips - 1, 1)
    share = rows // nt
    steps = max(nt.bit_length() - 1, 1)
    V = pltpu.VMEM
    dma = lambda *s: pltpu.SemaphoreType.DMA(s)
    scratch = [
        V((chips, 2 * rows, blk), BF16),
        V((nj, blk, 2 * cw), BF16),
        V((width, rank), BF16),
        V((width, oc), F32),
        V((2, 2 * rows, 2 * cw), F32),
        V((chips, nj, rows, 2 * cw), BF16),
        V((chips, nj, rows, 2 * cw), BF16),
        V((oth, nj, rows, 2 * cw), BF16),
        V((oth, nj, rows, 2 * cw), BF16),
        V((nj, rows, cw), BF16),
        V((rows, rank), F32),
        V((nt, share, rank), BF16),
        V((nt, share, rank), BF16),
        V((nt, share, rank), BF16),
        V((2, nj, chips, cw, oc), F32),
        V((2, nj, chips, cw, oc), BF16),
        V((nj, chips, cw, oc), BF16),
        V((oth, nj, cw, oc), BF16),
        V((oth, nj, cw, oc), BF16),
        dma(2), dma(2, nj), pltpu.SemaphoreType.DMA, pltpu.SemaphoreType.DMA, pltpu.SemaphoreType.DMA,
        dma(oth, 2), dma(oth, 2), dma(oth, 2, steps), dma(oth, 2, steps),
        dma(chips, nj), dma(chips, nj), dma(oth, nj), dma(oth, nj),
        dma(nt), dma(nt), dma(nt), dma(nt),
        dma(nj), dma(nj), dma(oth, nj), dma(oth, nj),
    ]
    return pl.pallas_call(
        functools.partial(kernel, ndp, nt, cw),
        out_shape=jax.ShapeDtypeStruct((width, oc), F32),
        in_specs=[pl.BlockSpec(memory_space=pl.ANY)] * 5,
        out_specs=pl.BlockSpec(memory_space=pltpu.VMEM),
        scratch_shapes=scratch,
        compiler_params=pltpu.CompilerParams(
            collective_id=0, has_side_effects=True, vmem_limit_bytes=60 * 1024 * 1024),
        cost_estimate=pl.CostEstimate(
            flops=4 * rows * ndp * blk * width, bytes_accessed=4 * blk * width, transcendentals=rows * width),
    )(tokens, gate_weight, up_weight, test_matrix, sketch_old)


def solution(mesh):
    in_specs = (
        P("dp", None),
        P("dp", "tensor"),
        P("dp", "tensor"),
        P("tensor", None),
        P("tensor", "dp"),
    )
    fn = functools.partial(local, mesh.shape["dp"], mesh.shape["tensor"])
    return jax.shard_map(fn, mesh=mesh, in_specs=in_specs, out_specs=P("tensor", "dp"), check_vma=False)
```

```python
import functools

import jax
import jax.numpy as jnp
from jax import lax
from jax.experimental import pallas as pl
from jax.experimental.pallas import tpu as pltpu
from jax.sharding import PartitionSpec as P

F32 = jnp.float32
BF16 = jnp.bfloat16


def kernel(
    ndp, nt, cw, tokens, wg, wu, test_hbm, old_hbm, out,
    xs, wv, test, old, acc, score, rcore, sy, ry, hid, proj, pstage, precv, pfull,
    u32, us, ur, us2, ur2,
    s_load, s_w, s_own, pt_s, pt_r, yt_s, yt_r, ag_s, ag_r, c_s, c_r, y_s, y_r,
    p_s, p_r, q_s, q_r, uc_s, uc_r, uy_s, uy_r,
):
    chips = ndp // 2
    rows = tokens.shape[0]
    blk, width = wg.shape
    nj = width // cw
    share = rows // nt
    steps = nt.bit_length() - 1
    d = lax.axis_index("dp")
    t = lax.axis_index("tensor")
    y = d // 2
    c = d % 2
    partner = 2 * y + 1 - c

    def rc(src, dst, ssem, rsem, dd, tt):
        return pltpu.make_async_remote_copy(
            src_ref=src, dst_ref=dst, send_sem=ssem, recv_sem=rsem,
            device_id=(dd, tt), device_id_type=pl.DeviceIdType.MESH,
        )

    def wload(j, h):
        src = (wg, wu)[h].at[:, pl.ds(pl.multiple_of(j * cw, cw), cw)]
        return pltpu.make_async_copy(src, wv.at[j, :, pl.ds(h * cw, cw)], s_w.at[h, j])

    own = pltpu.make_async_copy(
        tokens.at[:, pl.ds(pl.multiple_of(d * blk, blk), blk)],
        xs.at[y, pl.ds(pl.multiple_of(c * rows, rows), rows), :], s_own)
    own.start()
    for h in range(2):
        wload(0, h).start()

    barrier = pltpu.get_barrier_semaphore()
    for off in range(1, ndp):
        pl.semaphore_signal(barrier, inc=1, device_id=(lax.rem(d + off, ndp), t),
                            device_id_type=pl.DeviceIdType.MESH)
    for off in range(1, nt):
        pl.semaphore_signal(barrier, inc=1, device_id=(d, lax.rem(t + off, nt)),
                            device_id_type=pl.DeviceIdType.MESH)
    pl.semaphore_wait(barrier, ndp - 1 + nt - 1)

    orders = [[nt >> (k + 1) for k in range(steps)]]
    orders.append([1] + orders[0][:-1])

    def position(order):
        return sum(((t // b) % 2) * (1 << k) for k, b in enumerate(order))

    pos = [position(o) for o in orders]
    mypos = pos[0] * (1 - c) + pos[1] * c

    def region(s, cc, first, count):
        start = pl.multiple_of(cc * rows + first * share, share)
        return xs.at[s, pl.ds(start, count * share), :]

    to_partner = rc(
        tokens.at[:, pl.ds(pl.multiple_of(partner * blk, blk), blk)],
        xs.at[y, pl.ds(pl.multiple_of(c * rows, rows), rows), :],
        pt_s, pt_r, partner, t)
    to_partner.start()
    from_partner = rc(
        tokens.at[:, pl.ds(pl.multiple_of(partner * blk, blk), blk)],
        xs.at[y, pl.ds(pl.multiple_of((1 - c) * rows, rows), rows), :],
        pt_s, pt_r, partner, t)

    def token_send(i, e):
        q = 2 * lax.rem(y + i, chips) + lax.rem(c + e, 2)
        return rc(
            tokens.at[pl.ds(pl.multiple_of(mypos * share, share), share),
                      pl.ds(pl.multiple_of(q * blk, blk), blk)],
            region(y, c, mypos, 1), yt_s.at[i - 1, e], yt_r.at[i - 1, e], q, t)

    def token_recv(i, cc):
        s = lax.rem(y - i + chips, chips)
        e = lax.rem(c + cc, 2)
        ref = region(s, cc, pos[cc], 1)
        return rc(ref, ref, yt_s.at[i - 1, e], yt_r.at[i - 1, e], partner, t)

    for i in range(1, chips):
        for e in range(2):
            token_send(i, e).start()

    def gather_peer(cc, k):
        b = orders[cc][k]
        return t + (1 - 2 * ((t // b) % 2)) * b

    def gather_send(i, cc, k):
        s = lax.rem(y - i + chips, chips)
        first = (pos[cc] // (1 << k)) * (1 << k)
        ref = region(s, cc, first, 1 << k)
        return rc(ref, ref, ag_s.at[i - 1, cc, k], ag_r.at[i - 1, cc, k], d, gather_peer(cc, k))

    def gather_recv(i, cc, k):
        s = lax.rem(y - i + chips, chips)
        mine = pos[cc] // (1 << k)
        first = (mine + 1 - 2 * (mine % 2)) * (1 << k)
        ref = region(s, cc, first, 1 << k)
        return rc(ref, ref, ag_s.at[i - 1, cc, k], ag_r.at[i - 1, cc, k], d, gather_peer(cc, k))

    for j in range(1, nj):
        for h in range(2):
            wload(j, h).start()
    load_test = pltpu.make_async_copy(test_hbm, test, s_load.at[0])
    load_old = pltpu.make_async_copy(old_hbm, old, s_load.at[1])
    load_test.start()
    load_old.start()

    mine_rows = pl.ds(pl.multiple_of(c * rows, rows), rows)
    their_rows = pl.ds(pl.multiple_of((1 - c) * rows, rows), rows)

    def core_copy(i, j):
        return rc(score.at[i, j], rcore.at[i, j], c_s.at[i, j], c_r.at[i, j], partner, t)

    def y_copy(i, j):
        q = 2 * lax.rem(y + i + 1, chips) + c
        return rc(sy.at[i, j], ry.at[i, j], y_s.at[i, j], y_r.at[i, j], q, t)

    own.wait()
    from_partner.wait_recv()
    proj[...] = jnp.zeros_like(proj)
    half = 0
    second = min(3, nj - 1)

    for i in range(chips):
        s = lax.rem(y + i, chips)
        last = i == chips - 1

        def handle(j, i=i, last=last):
            core_copy(i, j).wait_recv()
            total = acc[j % 2, mine_rows, :] + rcore[i, j].astype(F32)
            if not last:
                sy[i, j] = total.astype(BF16)
                y_copy(i, j).start()
                return
            for k in range(chips - 1):
                y_copy(k, j).wait_recv()
                total = total + ry[k, j].astype(F32)
            gate = total[:, :cw]
            up = total[:, cw:]
            h = (gate / (1.0 + jnp.exp(-gate)) * up).astype(BF16)
            hid[j] = h
            proj[...] += jnp.dot(
                h, test[pl.ds(pl.multiple_of(j * cw, cw), cw), :], preferred_element_type=F32)

        if last:
            load_test.wait()

        def body(j, carry, i=i, s=s, handle=handle):
            if i == 0:
                for h in range(2):
                    wload(j, h).wait()
            acc[j % 2] = jnp.dot(xs[s], wv[j], preferred_element_type=F32)
            score[i, j] = acc[j % 2, their_rows, :].astype(BF16)
            core_copy(i, j).start()

            @pl.when(j > 0)
            def _():
                handle(j - 1)

            if i == 0 and chips > 1:
                @pl.when(j == half)
                def _():
                    for k in range(1, chips):
                        for cc in range(2):
                            token_recv(k, cc).wait_recv()
                            gather_send(k, cc, 0).start()

                @pl.when(j == second)
                def _():
                    for k in range(1, chips):
                        for cc in range(2):
                            gather_recv(k, cc, 0).wait_recv()
                            gather_send(k, cc, 1).start()
            return carry

        lax.fori_loop(0, nj, body, 0)
        handle(nj - 1)

        if i == 0 and chips > 1:
            for k in range(1, steps):
                for n in range(1, chips):
                    for cc in range(2):
                        gather_recv(n, cc, k).wait_recv()
                        if k + 1 < steps:
                            gather_send(n, cc, k + 1).start()

    for o in range(nt):
        pstage[o] = proj[o * share:(o + 1) * share, :].astype(BF16)

    def p_copy(off):
        tt = lax.rem(t + off, nt)
        return rc(pstage.at[tt], precv.at[off - 1], p_s.at[off - 1], p_r.at[off - 1], d, tt)

    def q_copy(off):
        tt = lax.rem(t + off, nt)
        return rc(pfull.at[t], pfull.at[t], q_s.at[off - 1], q_r.at[off - 1], d, tt)

    def q_recv(off):
        ref = pfull.at[lax.rem(t - off + nt, nt)]
        return rc(ref, ref, q_s.at[off - 1], q_r.at[off - 1], d, lax.rem(t + off, nt))

    for off in range(1, nt):
        p_copy(off).start()
    total = proj[pl.ds(pl.multiple_of(t * share, share), share), :]
    for off in range(1, nt):
        p_copy(off).wait_recv()
        total = total + precv[off - 1].astype(F32)
    pfull[t] = total.astype(BF16)
    for off in range(1, nt):
        q_copy(off).start()
    for off in range(1, nt):
        q_recv(off).wait_recv()

    oc = out.shape[1]

    def uc_copy(j):
        return rc(us.at[1 - c, j], ur.at[j], uc_s.at[j], uc_r.at[j], partner, t)

    def uy_copy(i, j):
        q = 2 * lax.rem(y + i, chips) + c
        return rc(us2.at[i - 1, j], ur2.at[i - 1, j], uy_s.at[i - 1, j], uy_r.at[i - 1, j], q, t)

    def u_handle(j):
        uc_copy(j).wait_recv()
        for i in range(1, chips):
            yy = lax.rem(y + i, chips)
            us2[i - 1, j] = (u32[c, j, yy] + ur[j, yy].astype(F32)).astype(BF16)
            uy_copy(i, j).start()

    def u_body(j, carry):
        full = pfull[...].reshape(rows, pfull.shape[2])
        r = lax.dot_general(hid[j], full, (((0,), (0,)), ((), ())), preferred_element_type=F32)
        for q in range(ndp):
            piece = r[:, q * oc:(q + 1) * oc]
            u32[q % 2, j, q // 2] = piece
            us[q % 2, j, q // 2] = piece.astype(BF16)
        uc_copy(j).start()

        @pl.when(j > 0)
        def _():
            u_handle(j - 1)
        return carry

    lax.fori_loop(0, nj, u_body, 0)
    u_handle(nj - 1)
    load_old.wait()
    scale = 1.0 / (rows * ndp)

    def o_body(j, carry):
        total = u32[c, j, y] + ur[j, y].astype(F32)
        for i in range(1, chips):
            uy_copy(i, j).wait_recv()
            total = total + ur2[i - 1, j].astype(F32)
        at = pl.ds(pl.multiple_of(j * cw, cw), cw)
        out[at, :] = old[at, :] + total * scale
        return carry

    lax.fori_loop(0, nj, o_body, 0)

    to_partner.wait_send()
    for i in range(1, chips):
        for e in range(2):
            token_send(i, e).wait_send()
            for k in range(steps):
                gather_send(i, e, k).wait_send()

    def w_body(j, carry):
        for i in range(chips):
            core_copy(i, j).wait_send()
            if i < chips - 1:
                y_copy(i, j).wait_send()
                uy_copy(i + 1, j).wait_send()
        uc_copy(j).wait_send()
        return carry

    lax.fori_loop(0, nj, w_body, 0)
    for off in range(1, nt):
        p_copy(off).wait_send()
        q_copy(off).wait_send()


def local(ndp, nt, tokens, gate_weight, up_weight, test_matrix, sketch_old):
    rows = tokens.shape[0]
    blk, width = gate_weight.shape
    rank = test_matrix.shape[1]
    oc = sketch_old.shape[1]
    cw = 256 if width % 256 == 0 else 128
    nj = width // cw
    chips = ndp // 2
    oth = max(chips - 1, 1)
    share = rows // nt
    steps = max(nt.bit_length() - 1, 1)
    V = pltpu.VMEM
    dma = lambda *s: pltpu.SemaphoreType.DMA(s)
    scratch = [
        V((chips, 2 * rows, blk), BF16),
        V((nj, blk, 2 * cw), BF16),
        V((width, rank), BF16),
        V((width, oc), F32),
        V((2, 2 * rows, 2 * cw), F32),
        V((chips, nj, rows, 2 * cw), BF16),
        V((chips, nj, rows, 2 * cw), BF16),
        V((oth, nj, rows, 2 * cw), BF16),
        V((oth, nj, rows, 2 * cw), BF16),
        V((nj, rows, cw), BF16),
        V((rows, rank), F32),
        V((nt, share, rank), BF16),
        V((nt, share, rank), BF16),
        V((nt, share, rank), BF16),
        V((2, nj, chips, cw, oc), F32),
        V((2, nj, chips, cw, oc), BF16),
        V((nj, chips, cw, oc), BF16),
        V((oth, nj, cw, oc), BF16),
        V((oth, nj, cw, oc), BF16),
        dma(2), dma(2, nj), pltpu.SemaphoreType.DMA, pltpu.SemaphoreType.DMA, pltpu.SemaphoreType.DMA,
        dma(oth, 2), dma(oth, 2), dma(oth, 2, steps), dma(oth, 2, steps),
        dma(chips, nj), dma(chips, nj), dma(oth, nj), dma(oth, nj),
        dma(nt), dma(nt), dma(nt), dma(nt),
        dma(nj), dma(nj), dma(oth, nj), dma(oth, nj),
    ]
    return pl.pallas_call(
        functools.partial(kernel, ndp, nt, cw),
        out_shape=jax.ShapeDtypeStruct((width, oc), F32),
        in_specs=[pl.BlockSpec(memory_space=pl.ANY)] * 5,
        out_specs=pl.BlockSpec(memory_space=pltpu.VMEM),
        scratch_shapes=scratch,
        compiler_params=pltpu.CompilerParams(
            collective_id=0, has_side_effects=True, vmem_limit_bytes=60 * 1024 * 1024),
        cost_estimate=pl.CostEstimate(
            flops=4 * rows * ndp * blk * width, bytes_accessed=4 * blk * width, transcendentals=rows * width),
    )(tokens, gate_weight, up_weight, test_matrix, sketch_old)


def solution(mesh):
    in_specs = (
        P("dp", None),
        P("dp", "tensor"),
        P("dp", "tensor"),
        P("tensor", None),
        P("tensor", "dp"),
    )
    fn = functools.partial(local, mesh.shape["dp"], mesh.shape["tensor"])
    return jax.shard_map(fn, mesh=mesh, in_specs=in_specs, out_specs=P("tensor", "dp"), check_vma=False)
```
